32 devices in a mesh: grp: 2 (over x), gz: 16 (over z, y, core).
Axes of the slice: x: 2, y: 2, z: 4, core: 2. Of those that a mesh axis runs over, the one named last changes fastest.
Arguments:
- sections: bfloat16 [256, 512, 256], P(('grp', 'gz')), parts along dimension 0, may hold values from -40 to 40, as said below
- radius: int32 [2], replicated, may hold values from 2 to 16
Outputs:
- ncc_maps: bfloat16 [256, 8, 512, 256], P(('grp', 'gz')), parts along dimension 0
- positions: float32 [256], P(('grp', 'gz')), parts along dimension 0
The draws below stay inside these ranges and needn't reach their ends.
There are 2 independent parts, one for each index of `grp`. The reference program is written for one: setup_inputs(seed, part) draws one part's arguments, and reference() takes and returns one part's arrays. A program takes and returns all parts, laid end to end along the dimension named above; an argument that names none is the same for every part. Nothing has to cross between parts.
Inputs may be any that keep to these rules, and one draw needn't show every extreme that they name: Rough from pixel to pixel; neighbouring sections are correlated.
All inputs are finite; a program needn't handle non-finite values.
Results may differ from the reference program's by a relative error of at most 0.0039.
Values may be sent and summed in bfloat16 or wider, within the bound.
A program may use at most 192 MiB of HBM per device.

```python
import jax
import jax.numpy as jnp
from jax import lax

TX = 512
TY = 256
REACH = 8
SECT_DEV = 8
NZ = 128


def draw_sections(key, part):
    key_noise, key_rho = jax.random.split(jax.random.fold_in(key, 71), 2)
    index = jnp.arange(NZ, dtype=jnp.int32)
    run_parity = index // SECT_DEV % 2
    base = jnp.where(run_parity == 0, jnp.float32(0.9), jnp.float32(0.3))
    rho = base + jax.random.uniform(key_rho, (NZ,), jnp.float32, -0.05, 0.05)
    noise = jax.random.normal(key_noise, (NZ, TX, TY), jnp.float32)

    def advance(state, item):
        coef, fresh = item
        state = coef * state + jnp.sqrt(1.0 - coef * coef) * fresh
        return (state, state)
    first = noise[0]
    rest_rho = rho[1:]
    _, later = lax.scan(advance, first, (rest_rho, noise[1:]))
    stack = jnp.concatenate([first[None], later], axis=0)
    return jnp.clip(stack, -40.0, 40.0).astype(jnp.bfloat16)


def setup_inputs(seed: int = 0, part: int = 0) -> dict:
    keys = jax.random.split(jax.random.key(seed), 3)
    part_keys = jax.random.split(jax.random.fold_in(keys[2], part), 3)
    sections = draw_sections(jax.random.fold_in(jax.random.fold_in(keys[2], part), 71), part)
    radius = jax.random.randint(keys[1], (2,), 2, 17).astype(jnp.int32)
    return {"sections": sections, "radius": radius}


def blur_table(count, radius_one):
    index = jnp.arange(count, dtype=jnp.int32)
    diff = index[:, None] - index[None, :]
    inside = jnp.abs(diff) <= radius_one
    sigma = radius_one.astype(jnp.float32) * 0.5
    dist = diff.astype(jnp.float32)
    table = jnp.where(inside, jnp.exp(-(dist * dist) / (2.0 * sigma * sigma)), jnp.float32(0.0))
    table = table / lax.optimization_barrier(jnp.sum(table, axis=1, keepdims=True))
    return table.astype(jnp.bfloat16)

def blur_one(single, gx, gy):
    half = jnp.dot(single, gy.T, preferred_element_type=jnp.float32).astype(jnp.bfloat16)
    return jnp.dot(gx, half, preferred_element_type=jnp.float32)

def blur_all(stack, gx, gy):
    return lax.map(lambda single: blur_one(single, gx, gy), stack)

def reference(sections, radius):
    gx = blur_table(TX, radius[0])
    gy = blur_table(TY, radius[1])
    ext = jnp.concatenate([sections, jnp.zeros((REACH, TX, TY), jnp.bfloat16)], axis=0)
    squares = (ext.astype(jnp.float32) * ext.astype(jnp.float32)).astype(jnp.bfloat16)
    mean_map = blur_all(ext, gx, gy)
    square_map = blur_all(squares, gx, gy)
    mu_a = mean_map[:NZ]
    var_a = square_map[:NZ] - mu_a * mu_a
    bands = []
    spacing = None
    for dist in range(1, REACH + 1):
        partner = ext[dist:dist + NZ]
        prod = (sections.astype(jnp.float32) * partner.astype(jnp.float32)).astype(jnp.bfloat16)
        mixed = blur_all(prod, gx, gy)
        mu_b = mean_map[dist:dist + NZ]
        var_b = square_map[dist:dist + NZ] - mu_b * mu_b
        ncc = (mixed - mu_a * mu_b) / jnp.sqrt((var_a + 0.1) * (var_b + 0.1))
        if dist == 1:
            spacing = 1.25 - lax.optimization_barrier(jnp.mean(ncc, axis=(1, 2)))
        bands.append(ncc.astype(jnp.bfloat16))
    ncc_maps = jnp.stack(bands, axis=1)
    positions = jnp.cumsum(spacing) * 0.015625
    return (ncc_maps, positions)
```

```python
import functools

import jax
import jax.numpy as jnp
from jax import lax
from jax.experimental import pallas as pl
from jax.experimental.pallas import tpu as pltpu
from jax.sharding import PartitionSpec as P

REACH = 8
MAX_RADIUS = 16
ROWS = 176
BATCH = 2
VMEM_LIMIT = 20 * 2**20


def windows(tx):
    width = min(256, tx)
    out = []
    start = 0
    while start < tx:
        rows = min(ROWS, tx - start)
        middle = (start + rows // 2 - width // 2) // 16 * 16
        low = min(max(middle, 0), tx - width)
        assert low == 0 or low <= start - MAX_RADIUS
        assert low + width == tx or low + width >= start + rows + MAX_RADIUS
        out.append((start, rows, low))
        start += rows
    return width, out


def table(radius, shape, first, second, axis):
    i = lax.broadcasted_iota(jnp.int32, shape, 0) + first
    j = lax.broadcasted_iota(jnp.int32, shape, 1) + second
    diff = i - j
    sigma = radius.astype(jnp.float32) * 0.5
    dist = diff.astype(jnp.float32)
    value = jnp.exp(-(dist * dist) / (2.0 * sigma * sigma))
    value = jnp.where(jnp.abs(diff) <= radius, value, 0.0)
    return (value / jnp.sum(value, axis=axis, keepdims=True)).astype(jnp.bfloat16)


def blur_to(half_ref, gx_ref, blocks, width, slot, finish):
    for start, rows, low in blocks:
        acc = jnp.dot(
            gx_ref[start : start + rows, :],
            half_ref[slot, low : low + width, :],
            preferred_element_type=jnp.float32,
        )
        finish(start, rows, acc)


def fill_moments(src_ref, count, mu_ref, inv_ref, gx_ref, gy_ref, half_ref, blocks, width):
    def step(r, _):
        x = src_ref[r]
        half_ref[0] = jnp.dot(x, gy_ref[...], preferred_element_type=jnp.float32).astype(
            jnp.bfloat16
        )
        half_ref[1] = jnp.dot(x * x, gy_ref[...], preferred_element_type=jnp.float32).astype(
            jnp.bfloat16
        )
        for start, rows, low in blocks:
            gx = gx_ref[start : start + rows, :]
            mu = jnp.dot(
                gx, half_ref[0, low : low + width, :], preferred_element_type=jnp.float32
            )
            sq = jnp.dot(
                gx, half_ref[1, low : low + width, :], preferred_element_type=jnp.float32
            )
            mu_ref[r, start : start + rows, :] = mu
            inv_ref[r, start : start + rows, :] = lax.rsqrt(jnp.abs(sq - mu * mu + 0.1))
        return 0

    lax.fori_loop(0, count, step, 0)


def fill_pairs(
    runs, src_ref, far_ref, mu_a, inv_a, mu_b, inv_b, gx_ref, gy_ref,
    half_ref, stage, sems, sums_ref, ncc_ref, blocks, width, count,
):
    total = runs[-1][0] + runs[-1][4]
    steps = total // BATCH
    assert steps * BATCH == total and steps >= 2

    def decode(q):
        slot, place, s = jnp.int32(0), jnp.int32(0), jnp.int32(0)
        for first, run_slot, run_place, low, _ in runs:
            here = q >= first
            slot = jnp.where(here, run_slot, slot)
            place = jnp.where(here, run_place, place)
            s = jnp.where(here, low + q - first, s)
        return slot, s, place - s

    def copy(bank, b, s, d):
        return pltpu.make_async_copy(
            stage.at[bank * BATCH + b], ncc_ref.at[s, d - 1], sems.at[bank * BATCH + b]
        )

    def step(t, _):
        bank = lax.rem(t, 2)
        which = [decode(t * BATCH + b) for b in range(BATCH)]

        @pl.when(t >= 2)
        def _():
            for b in range(BATCH):
                copy(bank, b, 0, 1).wait()

        for b, (slot, s, d) in enumerate(which):
            half_ref[b] = jnp.dot(
                src_ref[s] * far_ref[slot], gy_ref[...], preferred_element_type=jnp.float32
            ).astype(jnp.bfloat16)
        for b, (slot, s, d) in enumerate(which):
            parts = []

            def finish(start, rows, acc):
                at = slice(start, start + rows)
                ncc = (acc - mu_a[s, at, :] * mu_b[slot, at, :]) * (
                    inv_a[s, at, :] * inv_b[slot, at, :]
                )
                stage[bank * BATCH + b, at, :] = ncc.astype(jnp.bfloat16)
                parts.append(jnp.sum(ncc.reshape(rows // 8, 8, ncc.shape[1]), axis=0))

            blur_to(half_ref, gx_ref, blocks, width, b, finish)
            sums_ref[jnp.where(d == 1, s, count)] = functools.reduce(jnp.add, parts)
            copy(bank, b, s, d).start()
        return 0

    lax.fori_loop(0, steps, step, 0)
    for bank in range(2):
        for b in range(BATCH):
            copy(bank, b, 0, 1).wait()


def local_kernel(
    blocks, width, runs, count,
    radius_ref, src_ref,
    ncc_ref, sums_ref, mu_ref, inv_ref, gx_ref, gy_ref,
    half_ref, stage, sems,
):
    for start, rows, low in blocks:
        gx_ref[start : start + rows, :] = table(radius_ref[0], (rows, width), start, low, 1)
    gy_ref[...] = table(radius_ref[1], gy_ref.shape, 0, 0, 0)
    fill_moments(src_ref, count, mu_ref, inv_ref, gx_ref, gy_ref, half_ref, blocks, width)
    fill_pairs(
        runs, src_ref, src_ref, mu_ref, inv_ref, mu_ref, inv_ref, gx_ref, gy_ref,
        half_ref, stage, sems, sums_ref, ncc_ref, blocks, width, count,
    )


def far_kernel(
    blocks, width, runs, count,
    src_ref, far_ref, mu_ref, inv_ref, gx_ref, gy_ref, old_ref,
    ncc_ref, sums_ref,
    mu_far, inv_far, half_ref, stage, sems,
):
    fill_moments(
        far_ref, far_ref.shape[0], mu_far, inv_far, gx_ref, gy_ref, half_ref, blocks, width
    )
    fill_pairs(
        runs, src_ref, far_ref, mu_ref, inv_ref, mu_far, inv_far, gx_ref, gy_ref,
        half_ref, stage, sems, sums_ref, ncc_ref, blocks, width, count,
    )


def make_runs(places, count):
    out = []
    first = 0
    for slot, place in places:
        low, high = max(0, place - REACH), min(place, count)
        if high > low:
            out.append((first, slot, place, low, high - low))
            first += high - low
    return out


def per_device(sections, radius):
    count, tx, ty = sections.shape
    width, blocks = windows(tx)
    axis = lax.axis_size("gz")
    back = [(i, i - 1) for i in range(1, axis)]
    cuts = [0, 1, 4, REACH]
    received = [
        lax.ppermute(sections[a:b], "gz", back) for a, b in zip(cuts[:-1], cuts[1:])
    ]
    vmem = pl.BlockSpec(memory_space=pltpu.VMEM)
    smem = pl.BlockSpec(memory_space=pltpu.SMEM)
    hbm = pl.BlockSpec(memory_space=pl.ANY)
    shape = jax.ShapeDtypeStruct
    ncc_type = shape((count, REACH, tx, ty), jnp.bfloat16)
    sums_type = shape((count + 1, 8, ty), jnp.float32)
    map_type = shape((count, tx, ty), jnp.float32)
    work = [
        pltpu.VMEM((2, tx, ty), jnp.bfloat16),
        pltpu.VMEM((2 * BATCH, tx, ty), jnp.bfloat16),
        pltpu.SemaphoreType.DMA((2 * BATCH,)),
    ]
    params = pltpu.CompilerParams(vmem_limit_bytes=VMEM_LIMIT)

    def cost(maps):
        return pl.CostEstimate(
            flops=maps * 2 * tx * ty * (ty + width),
            bytes_accessed=maps * tx * ty * 2,
            transcendentals=0,
        )

    runs = make_runs([(p, p) for p in range(count)], count)
    ncc, sums, mu, inv, gx, gy = pl.pallas_call(
        functools.partial(local_kernel, blocks, width, runs, count),
        out_shape=(
            ncc_type, sums_type, map_type, map_type,
            shape((tx, width), jnp.bfloat16), shape((ty, ty), jnp.bfloat16),
        ),
        in_specs=[smem, vmem],
        out_specs=(hbm, vmem, vmem, vmem, vmem, vmem),
        scratch_shapes=work,
        compiler_params=params,
        cost_estimate=cost(44),
        name="local_pairs",
    )(radius, sections)
    near = jnp.sum(sums[: count - 1], axis=(1, 2))
    positions = None
    for k, (a, b) in enumerate(zip(cuts[:-1], cuts[1:])):
        runs = make_runs([(j - a, count + j) for j in range(a, b)], count)
        ncc, sums = pl.pallas_call(
            functools.partial(far_kernel, blocks, width, runs, count),
            out_shape=(ncc_type, sums_type),
            in_specs=[vmem] * 6 + [hbm],
            out_specs=(hbm, vmem),
            scratch_shapes=[pltpu.VMEM((b - a, tx, ty), jnp.float32)] * 2 + work,
            input_output_aliases={6: 0},
            compiler_params=params,
            cost_estimate=cost(sum(r[4] for r in runs) + 2 * (b - a)),
            name=f"far_pairs_{k}",
        )(sections, received[k], mu, inv, gx, gy, ncc)
        if k == 0:
            last = jnp.sum(sums[count - 1 : count], axis=(1, 2))
            spacing = 1.25 - jnp.concatenate([near, last]) / (tx * ty)
            every = lax.all_gather(jnp.sum(spacing, keepdims=True), "gz", axis=0, tiled=True)
            earlier = jnp.arange(axis, dtype=jnp.int32) < lax.axis_index("gz")
            before = jnp.sum(jnp.where(earlier, every, 0.0))
            order = jnp.arange(count, dtype=jnp.int32)
            running = jnp.sum(
                jnp.where(order[None, :] <= order[:, None], spacing[None, :], 0.0), axis=1
            )
            positions = (running + before) * 0.015625
    return (ncc, positions)


def solution(mesh):
    in_specs = (P(("grp", "gz"), None, None), P())
    out_specs = (P(("grp", "gz"), None, None, None), P(("grp", "gz")))
    return jax.shard_map(
        per_device, mesh=mesh, in_specs=in_specs, out_specs=out_specs, check_vma=False
    )
```

```python
import functools

import jax
import jax.numpy as jnp
from jax import lax
from jax.experimental import pallas as pl
from jax.experimental.pallas import tpu as pltpu
from jax.sharding import PartitionSpec as P

REACH = 8
MAX_RADIUS = 16
LANES = 128
ROWS = 176
BATCH = 2
VMEM_LIMIT = 26 * 2**20


def windows(tx):
    width = min(256, tx)
    out = []
    start = 0
    while start < tx:
        rows = min(ROWS, tx - start)
        middle = (start + rows // 2 - width // 2) // 16 * 16
        low = min(max(middle, 0), tx - width)
        assert low == 0 or low <= start - MAX_RADIUS
        assert low + width == tx or low + width >= start + rows + MAX_RADIUS
        out.append((start, rows, low))
        start += rows
    return width, out


def table(radius, shape, first, second, axis):
    i = lax.broadcasted_iota(jnp.int32, shape, 0) + first
    j = lax.broadcasted_iota(jnp.int32, shape, 1) + second
    diff = i - j
    sigma = radius.astype(jnp.float32) * 0.5
    dist = diff.astype(jnp.float32)
    value = jnp.exp(-(dist * dist) / (2.0 * sigma * sigma))
    value = jnp.where(jnp.abs(diff) <= radius, value, 0.0)
    return (value / jnp.sum(value, axis=axis, keepdims=True)).astype(jnp.bfloat16)


def blur_to(half_ref, gx_ref, blocks, width, slot, finish):
    for start, rows, low in blocks:
        acc = jnp.dot(
            gx_ref[start : start + rows, :],
            half_ref[slot, low : low + width, :],
            preferred_element_type=jnp.float32,
        )
        finish(start, rows, acc)


def fill_moments(src_ref, count, mu_ref, inv_ref, gx_ref, gy_ref, half_ref, blocks, width):
    def step(r, _):
        x = src_ref[r]
        half_ref[0] = jnp.dot(x, gy_ref[...], preferred_element_type=jnp.float32).astype(
            jnp.bfloat16
        )
        half_ref[1] = jnp.dot(x * x, gy_ref[...], preferred_element_type=jnp.float32).astype(
            jnp.bfloat16
        )
        for start, rows, low in blocks:
            gx = gx_ref[start : start + rows, :]
            mu = jnp.dot(
                gx, half_ref[0, low : low + width, :], preferred_element_type=jnp.float32
            )
            sq = jnp.dot(
                gx, half_ref[1, low : low + width, :], preferred_element_type=jnp.float32
            )
            mu_ref[r, start : start + rows, :] = mu
            inv_ref[r, start : start + rows, :] = lax.rsqrt(jnp.abs(sq - mu * mu + 0.1))
        return 0

    lax.fori_loop(0, count, step, 0)


def fill_pairs(
    runs, src_ref, far_ref, mu_a, inv_a, mu_b, inv_b, gx_ref, gy_ref,
    half_ref, stage, sems, sums_ref, ncc_ref, blocks, width, count,
):
    total = runs[-1][0] + runs[-1][4]
    steps = total // BATCH
    assert steps * BATCH == total and steps >= 2

    def decode(q):
        slot, place, s = jnp.int32(0), jnp.int32(0), jnp.int32(0)
        for first, run_slot, run_place, low, _ in runs:
            here = q >= first
            slot = jnp.where(here, run_slot, slot)
            place = jnp.where(here, run_place, place)
            s = jnp.where(here, low + q - first, s)
        return slot, s, place - s

    def copy(bank, b, s, d):
        return pltpu.make_async_copy(
            stage.at[bank * BATCH + b], ncc_ref.at[s, d - 1], sems.at[bank * BATCH + b]
        )

    def step(t, _):
        bank = lax.rem(t, 2)
        which = [decode(t * BATCH + b) for b in range(BATCH)]

        @pl.when(t >= 2)
        def _():
            for b in range(BATCH):
                copy(bank, b, 0, 1).wait()

        for b, (slot, s, d) in enumerate(which):
            half_ref[b] = jnp.dot(
                src_ref[s] * far_ref[slot], gy_ref[...], preferred_element_type=jnp.float32
            ).astype(jnp.bfloat16)
        for b, (slot, s, d) in enumerate(which):
            parts = []

            def finish(start, rows, acc):
                at = slice(start, start + rows)
                ncc = (acc - mu_a[s, at, :] * mu_b[slot, at, :]) * (
                    inv_a[s, at, :] * inv_b[slot, at, :]
                )
                stage[bank * BATCH + b, at, :] = ncc.astype(jnp.bfloat16)
                parts.append(jnp.sum(ncc.reshape(rows // 8, 8, ncc.shape[1]), axis=0))

            blur_to(half_ref, gx_ref, blocks, width, b, finish)
            sums_ref[jnp.where(d == 1, s, count)] = functools.reduce(jnp.add, parts)
            copy(bank, b, s, d).start()
        return 0

    lax.fori_loop(0, steps, step, 0)
    for bank in range(2):
        for b in range(BATCH):
            copy(bank, b, 0, 1).wait()


def local_kernel(
    blocks, width, runs, count,
    radius_ref, src_ref,
    ncc_ref, sums_ref, mu_ref, inv_ref, gx_ref, gy_ref,
    half_ref, stage, sems,
):
    for start, rows, low in blocks:
        gx_ref[start : start + rows, :] = table(radius_ref[0], (rows, width), start, low, 1)
    gy_ref[...] = table(radius_ref[1], gy_ref.shape, 0, 0, 0)
    fill_moments(src_ref, count, mu_ref, inv_ref, gx_ref, gy_ref, half_ref, blocks, width)
    fill_pairs(
        runs, src_ref, src_ref, mu_ref, inv_ref, mu_ref, inv_ref, gx_ref, gy_ref,
        half_ref, stage, sems, sums_ref, ncc_ref, blocks, width, count,
    )


def far_kernel(
    blocks, width, runs, count,
    src_ref, far_ref, mu_ref, inv_ref, gx_ref, gy_ref, old_ref,
    ncc_ref, sums_ref,
    mu_far, inv_far, half_ref, stage, sems,
):
    fill_moments(
        far_ref, far_ref.shape[0], mu_far, inv_far, gx_ref, gy_ref, half_ref, blocks, width
    )
    fill_pairs(
        runs, src_ref, far_ref, mu_ref, inv_ref, mu_far, inv_far, gx_ref, gy_ref,
        half_ref, stage, sems, sums_ref, ncc_ref, blocks, width, count,
    )


def share_kernel(
    devices, count, pixels, near_ref, far_ref, out_ref, mine, slots, send_sems, recv_sems
):
    me = lax.axis_index("gz")
    barrier = pltpu.get_barrier_semaphore()
    peers = [lax.rem(me + k, devices) for k in range(1, devices)]
    for peer in peers:
        pl.semaphore_signal(
            barrier, inc=1, device_id={"gz": peer}, device_id_type=pl.DeviceIdType.MESH
        )
    near = jnp.sum(jnp.sum(near_ref[:count], axis=1), axis=1, keepdims=True)
    last = jnp.sum(jnp.sum(far_ref[count - 1 : count], axis=1), axis=1, keepdims=True)
    row = lax.broadcasted_iota(jnp.int32, (count, LANES), 0)
    lane = lax.broadcasted_iota(jnp.int32, (count, LANES), 1)
    sums = jnp.where(row < count - 1, near, last)
    spacing = 1.25 - sums / pixels
    mine[...] = jnp.broadcast_to(jnp.sum(spacing, axis=0, keepdims=True), mine.shape)
    running = jnp.sum(jnp.where(row <= lane, spacing, 0.0), axis=0, keepdims=True)
    pl.semaphore_wait(barrier, devices - 1)
    copies = []
    for k, peer in enumerate(peers, 1):
        copy = pltpu.make_async_remote_copy(
            src_ref=mine,
            dst_ref=slots.at[k],
            send_sem=send_sems.at[k],
            recv_sem=recv_sems.at[k],
            device_id={"gz": peer},
            device_id_type=pl.DeviceIdType.MESH,
        )
        copy.start()
        copies.append(copy)
    for copy in copies:
        copy.wait()
    for k in range(1, devices):
        running = running + jnp.where(k <= me, slots[k, :1, :], 0.0)
    out_ref[...] = running * 0.015625


def make_runs(places, count):
    out = []
    first = 0
    for slot, place in places:
        low, high = max(0, place - REACH), min(place, count)
        if high > low:
            out.append((first, slot, place, low, high - low))
            first += high - low
    return out


def per_device(sections, radius):
    count, tx, ty = sections.shape
    width, blocks = windows(tx)
    axis = lax.axis_size("gz")
    back = [(i, i - 1) for i in range(1, axis)]
    received = lax.ppermute(sections, "gz", back)
    vmem = pl.BlockSpec(memory_space=pltpu.VMEM)
    smem = pl.BlockSpec(memory_space=pltpu.SMEM)
    hbm = pl.BlockSpec(memory_space=pl.ANY)
    shape = jax.ShapeDtypeStruct
    ncc_type = shape((count, REACH, tx, ty), jnp.bfloat16)
    sums_type = shape((count + 1, 8, ty), jnp.float32)
    map_type = shape((count, tx, ty), jnp.float32)
    work = [
        pltpu.VMEM((2, tx, ty), jnp.bfloat16),
        pltpu.VMEM((2 * BATCH, tx, ty), jnp.bfloat16),
        pltpu.SemaphoreType.DMA((2 * BATCH,)),
    ]
    params = pltpu.CompilerParams(vmem_limit_bytes=VMEM_LIMIT)

    def cost(maps):
        return pl.CostEstimate(
            flops=maps * 2 * tx * ty * (ty + width),
            bytes_accessed=maps * tx * ty * 2,
            transcendentals=0,
        )

    runs = make_runs([(p, p) for p in range(count)], count)
    ncc, sums, mu, inv, gx, gy = pl.pallas_call(
        functools.partial(local_kernel, blocks, width, runs, count),
        out_shape=(
            ncc_type, sums_type, map_type, map_type,
            shape((tx, width), jnp.bfloat16), shape((ty, ty), jnp.bfloat16),
        ),
        in_specs=[smem, vmem],
        out_specs=(hbm, vmem, vmem, vmem, vmem, vmem),
        scratch_shapes=work,
        compiler_params=params,
        cost_estimate=cost(44),
        name="local_pairs",
    )(radius, sections)
    runs = make_runs([(j, count + j) for j in range(REACH)], count)
    ncc, sums_far = pl.pallas_call(
        functools.partial(far_kernel, blocks, width, runs, count),
        out_shape=(ncc_type, sums_type),
        in_specs=[vmem] * 6 + [hbm],
        out_specs=(hbm, vmem),
        scratch_shapes=[pltpu.VMEM((REACH, tx, ty), jnp.float32)] * 2 + work,
        input_output_aliases={6: 0},
        compiler_params=params,
        cost_estimate=cost(52),
        name="far_pairs",
    )(sections, received, mu, inv, gx, gy, ncc)
    positions = pl.pallas_call(
        functools.partial(share_kernel, axis, count, tx * ty),
        out_shape=shape((1, LANES), jnp.float32),
        in_specs=[vmem] * 2,
        out_specs=vmem,
        scratch_shapes=[
            pltpu.VMEM((8, LANES), jnp.float32),
            pltpu.VMEM((axis, 8, LANES), jnp.float32),
            pltpu.SemaphoreType.DMA((axis,)),
            pltpu.SemaphoreType.DMA((axis,)),
        ],
        compiler_params=pltpu.CompilerParams(collective_id=0, has_side_effects=True),
        name="share_totals",
    )(sums, sums_far)
    return (ncc, positions[0, :count])


def solution(mesh):
    in_specs = (P(("grp", "gz"), None, None), P())
    out_specs = (P(("grp", "gz"), None, None, None), P(("grp", "gz")))
    return jax.shard_map(
        per_device, mesh=mesh, in_specs=in_specs, out_specs=out_specs, check_vma=False
    )
```

```python
import functools

import jax
import jax.numpy as jnp
from jax import lax
from jax.experimental import pallas as pl
from jax.experimental.pallas import tpu as pltpu
from jax.sharding import PartitionSpec as P

REACH = 8
MAX_RADIUS = 16
LANES = 128
ROWS = 176
BATCH = 2
LATE = 4
FIRST_LIMIT = 24 * 2**20
LAST_LIMIT = 18 * 2**20


def windows(tx):
    width = min(256, tx)
    out = []
    start = 0
    while start < tx:
        rows = min(ROWS, tx - start)
        middle = (start + rows // 2 - width // 2) // 16 * 16
        low = min(max(middle, 0), tx - width)
        assert low == 0 or low <= start - MAX_RADIUS
        assert low + width == tx or low + width >= start + rows + MAX_RADIUS
        out.append((start, rows, low))
        start += rows
    return width, out


def table(radius, shape, first, second, axis):
    i = lax.broadcasted_iota(jnp.int32, shape, 0) + first
    j = lax.broadcasted_iota(jnp.int32, shape, 1) + second
    diff = i - j
    sigma = radius.astype(jnp.float32) * 0.5
    dist = diff.astype(jnp.float32)
    value = jnp.exp(-(dist * dist) / (2.0 * sigma * sigma))
    value = jnp.where(jnp.abs(diff) <= radius, value, 0.0)
    return (value / jnp.sum(value, axis=axis, keepdims=True)).astype(jnp.bfloat16)


def blur_to(half_ref, gx_ref, blocks, width, slot, finish):
    for start, rows, low in blocks:
        acc = jnp.dot(
            gx_ref[start : start + rows, :],
            half_ref[slot, low : low + width, :],
            preferred_element_type=jnp.float32,
        )
        finish(start, rows, acc)


def fill_moments(src_ref, count, mu_ref, inv_ref, gx_ref, gy_ref, half_ref, blocks, width):
    def step(r, _):
        x = src_ref[r]
        half_ref[0] = jnp.dot(x, gy_ref[...], preferred_element_type=jnp.float32).astype(
            jnp.bfloat16
        )
        half_ref[1] = jnp.dot(x * x, gy_ref[...], preferred_element_type=jnp.float32).astype(
            jnp.bfloat16
        )
        for start, rows, low in blocks:
            gx = gx_ref[start : start + rows, :]
            mu = jnp.dot(
                gx, half_ref[0, low : low + width, :], preferred_element_type=jnp.float32
            )
            sq = jnp.dot(
                gx, half_ref[1, low : low + width, :], preferred_element_type=jnp.float32
            )
            mu_ref[r, start : start + rows, :] = mu
            inv_ref[r, start : start + rows, :] = lax.rsqrt(jnp.abs(sq - mu * mu + 0.1))
        return 0

    lax.fori_loop(0, count, step, 0)


def fill_pairs(
    runs, src_ref, far_ref, mu_a, inv_a, mu_b, inv_b, gx_ref, gy_ref,
    half_ref, stage, sems, sums_ref, ncc_ref, blocks, width, count, early=None, base=0,
):
    total = runs[-1][0] + runs[-1][4]
    steps = total // BATCH
    assert steps * BATCH == total and steps >= 2

    def decode(q):
        slot, place, s = jnp.int32(0), jnp.int32(0), jnp.int32(0)
        for first, run_slot, run_place, low, _ in runs:
            here = q >= first
            slot = jnp.where(here, run_slot, slot)
            place = jnp.where(here, run_place, place)
            s = jnp.where(here, low + q - first, s)
        return slot, s, place - s

    def copy(bank, b, s, d):
        return pltpu.make_async_copy(
            stage.at[bank * BATCH + b], ncc_ref.at[s, d - 1], sems.at[bank * BATCH + b]
        )

    def step(t, _):
        bank = lax.rem(t, 2)
        which = [decode(t * BATCH + b) for b in range(BATCH)]

        if early is None:

            @pl.when(t >= 2)
            def _():
                for b in range(BATCH):
                    copy(bank, b, 0, 1).wait()

        for b, (slot, s, d) in enumerate(which):
            half_ref[b] = jnp.dot(
                src_ref[s] * far_ref[slot], gy_ref[...], preferred_element_type=jnp.float32
            ).astype(jnp.bfloat16)
        for b, (slot, s, d) in enumerate(which):
            parts = []

            def finish(start, rows, acc):
                at = slice(start, start + rows)
                ncc = (acc - mu_a[s, at, :] * mu_b[slot, at, :]) * (
                    inv_a[s, at, :] * inv_b[slot, at, :]
                )
                if early is None:
                    stage[bank * BATCH + b, at, :] = ncc.astype(jnp.bfloat16)
                else:
                    early[base + t * BATCH + b, at, :] = ncc.astype(jnp.bfloat16)
                    parts.append(jnp.sum(ncc.reshape(rows // 8, 8, ncc.shape[1]), axis=0))

            blur_to(half_ref, gx_ref, blocks, width, b, finish)
            if early is None:
                copy(bank, b, s, d).start()
            else:
                sums_ref[jnp.where(d == 1, s, count)] = functools.reduce(jnp.add, parts)
        return 0

    lax.fori_loop(0, steps, step, 0)
    if early is not None:
        return
    for bank in range(2):
        for b in range(BATCH):
            copy(bank, b, 0, 1).wait()


def first_kernel(
    blocks, width, groups, count, devices, pixels,
    radius_ref, src_ref,
    early_ref, far_ref, mu_ref, inv_ref, gx_ref, gy_ref, out_ref,
    mu_far, inv_far, half_ref, sums_ref, mine, slots,
    halo_send, halo_recv, send_sems, recv_sems,
):
    me = lax.axis_index("gz")
    mesh_id = pl.DeviceIdType.MESH
    barrier = pltpu.get_barrier_semaphore()
    peers = [lax.rem(me + k, devices) for k in range(1, devices)]
    for peer in peers:
        pl.semaphore_signal(barrier, inc=1, device_id={"gz": peer}, device_id_type=mesh_id)
    for start, rows, low in blocks:
        gx_ref[start : start + rows, :] = table(radius_ref[0], (rows, width), start, low, 1)
    gy_ref[...] = table(radius_ref[1], gy_ref.shape, 0, 0, 0)
    pl.semaphore_wait(barrier, devices - 1)
    halo = [
        pltpu.make_async_remote_copy(
            src_ref=src_ref.at[j],
            dst_ref=far_ref.at[j],
            send_sem=halo_send.at[j],
            recv_sem=halo_recv.at[j],
            device_id={"gz": lax.rem(me + devices - 1, devices)},
            device_id_type=mesh_id,
        )
        for j in range(REACH)
    ]

    @pl.when(me > 0)
    def _():
        for copy in halo:
            copy.start()

    def arrive(a, b):
        @pl.when(me < devices - 1)
        def _():
            for j in range(a, b):
                halo[j].wait_recv()

        @pl.when(me == devices - 1)
        def _():
            for j in range(a, b):
                far_ref[j] = jnp.zeros(far_ref.shape[1:], far_ref.dtype)

    fill_moments(src_ref, count, mu_ref, inv_ref, gx_ref, gy_ref, half_ref, blocks, width)
    base, copies, running = 0, [], None
    for a, b, runs in groups:
        if b == 0:
            source, mu_b, inv_b = src_ref, mu_ref, inv_ref
        else:
            arrive(a, b)
            source, mu_b, inv_b = far_ref.at[pl.ds(a, b - a)], mu_far, inv_far
            fill_moments(
                source, b - a, mu_far, inv_far, gx_ref, gy_ref, half_ref, blocks, width
            )
        fill_pairs(
            runs, src_ref, source, mu_ref, inv_ref, mu_b, inv_b, gx_ref, gy_ref,
            half_ref, None, None, sums_ref, None, blocks, width, count, early_ref, base,
        )
        base += runs[-1][0] + runs[-1][4]
        if b == 1:
            sums = jnp.sum(jnp.sum(sums_ref[:count], axis=1), axis=1, keepdims=True)
            row = lax.broadcasted_iota(jnp.int32, (count, LANES), 0)
            lane = lax.broadcasted_iota(jnp.int32, (count, LANES), 1)
            spacing = 1.25 - jnp.broadcast_to(sums, (count, LANES)) / pixels
            mine[...] = jnp.broadcast_to(jnp.sum(spacing, axis=0, keepdims=True), mine.shape)
            running = jnp.sum(jnp.where(row <= lane, spacing, 0.0), axis=0, keepdims=True)
            for k, peer in enumerate(peers, 1):
                copy = pltpu.make_async_remote_copy(
                    src_ref=mine,
                    dst_ref=slots.at[k],
                    send_sem=send_sems.at[k],
                    recv_sem=recv_sems.at[k],
                    device_id={"gz": peer},
                    device_id_type=mesh_id,
                )
                copy.start()
                copies.append(copy)
    arrive(groups[-1][1], REACH)

    @pl.when(me > 0)
    def _():
        for copy in halo:
            copy.wait_send()

    for copy in copies:
        copy.wait()
    for k in range(1, devices):
        running = running + jnp.where(k <= me, slots[k, :1, :], 0.0)
    out_ref[...] = running * 0.015625


def last_kernel(
    blocks, width, groups, runs, begin, count,
    src_ref, far_ref, mu_ref, inv_ref, gx_ref, gy_ref, early_ref,
    ncc_ref,
    mu_far, inv_far, half_ref, stage, sems, early_sems,
):
    copies = []
    for _, _, done in groups:
        for _, _, place, low, number in done:
            for s in range(low, low + number):
                q = len(copies)
                copy = pltpu.make_async_copy(
                    early_ref.at[q], ncc_ref.at[s, place - s - 1], early_sems.at[q]
                )
                copy.start()
                copies.append(copy)
    source = far_ref.at[pl.ds(begin, REACH - begin)]
    fill_moments(
        source, REACH - begin, mu_far, inv_far, gx_ref, gy_ref, half_ref, blocks, width
    )
    fill_pairs(
        runs, src_ref, source, mu_ref, inv_ref, mu_far, inv_far, gx_ref, gy_ref,
        half_ref, stage, sems, None, ncc_ref, blocks, width, count,
    )
    for copy in copies:
        copy.wait()


def make_runs(places, count):
    out = []
    first = 0
    for slot, place in places:
        low, high = max(0, place - REACH), min(place, count)
        if high > low:
            out.append((first, slot, place, low, high - low))
            first += high - low
    return out


def per_device(sections, radius):
    count, tx, ty = sections.shape
    width, blocks = windows(tx)
    axis = lax.axis_size("gz")
    vmem = pl.BlockSpec(memory_space=pltpu.VMEM)
    smem = pl.BlockSpec(memory_space=pltpu.SMEM)
    hbm = pl.BlockSpec(memory_space=pl.ANY)
    shape = jax.ShapeDtypeStruct
    map_type = shape((count, tx, ty), jnp.float32)
    groups = [(0, 0, make_runs([(p, p) for p in range(count)], count))]
    for a, b in ((0, 1), (1, LATE)):
        groups.append((a, b, make_runs([(j - a, count + j) for j in range(a, b)], count)))
    late = make_runs([(j - LATE, count + j) for j in range(LATE, REACH)], count)
    pairs = sum(runs[-1][0] + runs[-1][4] for _, _, runs in groups)
    dma = pltpu.SemaphoreType.DMA
    early, far, mu, inv, gx, gy, positions = pl.pallas_call(
        functools.partial(first_kernel, blocks, width, groups, count, axis, tx * ty),
        out_shape=(
            shape((pairs, tx, ty), jnp.bfloat16),
            shape((REACH, tx, ty), jnp.bfloat16),
            map_type, map_type,
            shape((tx, width), jnp.bfloat16), shape((ty, ty), jnp.bfloat16),
            shape((1, LANES), jnp.float32),
        ),
        in_specs=[smem, vmem],
        out_specs=[vmem] * 7,
        scratch_shapes=[pltpu.VMEM((LATE - 1, tx, ty), jnp.float32)] * 2
        + [
            pltpu.VMEM((2, tx, ty), jnp.bfloat16),
            pltpu.VMEM((count + 1, 8, ty), jnp.float32),
            pltpu.VMEM((8, LANES), jnp.float32),
            pltpu.VMEM((axis, 8, LANES), jnp.float32),
            dma((REACH,)), dma((REACH,)), dma((axis,)), dma((axis,)),
        ],
        compiler_params=pltpu.CompilerParams(
            collective_id=0, has_side_effects=True, vmem_limit_bytes=FIRST_LIMIT
        ),
        name="first_pairs",
    )(radius, sections)
    ncc = pl.pallas_call(
        functools.partial(last_kernel, blocks, width, groups, late, LATE, count),
        out_shape=shape((count, REACH, tx, ty), jnp.bfloat16),
        in_specs=[vmem] * 6 + [hbm],
        out_specs=hbm,
        scratch_shapes=[pltpu.VMEM((REACH - LATE, tx, ty), jnp.float32)] * 2
        + [
            pltpu.VMEM((2, tx, ty), jnp.bfloat16),
            pltpu.VMEM((2 * BATCH, tx, ty), jnp.bfloat16),
            dma((2 * BATCH,)), dma((pairs,)),
        ],
        compiler_params=pltpu.CompilerParams(vmem_limit_bytes=LAST_LIMIT),
        name="last_pairs",
    )(sections, far, mu, inv, gx, gy, early)
    return (ncc, positions[0, :count])


def solution(mesh):
    in_specs = (P(("grp", "gz"), None, None), P())
    out_specs = (P(("grp", "gz"), None, None, None), P(("grp", "gz")))
    return jax.shard_map(
        per_device, mesh=mesh, in_specs=in_specs, out_specs=out_specs, check_vma=False
    )
```

```python
import functools

import jax
import jax.numpy as jnp
from jax import lax
from jax.experimental import pallas as pl
from jax.experimental.pallas import tpu as pltpu
from jax.sharding import PartitionSpec as P

REACH = 8
MAX_RADIUS = 16
LANES = 128
ROWS = 176
BATCH = 2
LATE = 4
FIRST_LIMIT = 24 * 2**20
LAST_LIMIT = 18 * 2**20


def windows(tx):
    width = min(256, tx)
    out = []
    start = 0
    while start < tx:
        rows = min(ROWS, tx - start)
        middle = (start + rows // 2 - width // 2) // 16 * 16
        low = min(max(middle, 0), tx - width)
        assert low == 0 or low <= start - MAX_RADIUS
        assert low + width == tx or low + width >= start + rows + MAX_RADIUS
        out.append((start, rows, low))
        start += rows
    return width, out


def table(radius, shape, first, second, axis):
    i = lax.broadcasted_iota(jnp.int32, shape, 0) + first
    j = lax.broadcasted_iota(jnp.int32, shape, 1) + second
    diff = i - j
    sigma = radius.astype(jnp.float32) * 0.5
    dist = diff.astype(jnp.float32)
    value = jnp.exp(-(dist * dist) / (2.0 * sigma * sigma))
    value = jnp.where(jnp.abs(diff) <= radius, value, 0.0)
    return (value / jnp.sum(value, axis=axis, keepdims=True)).astype(jnp.bfloat16)


def blur_to(half_ref, gx_ref, blocks, width, slot, finish):
    for start, rows, low in blocks:
        acc = jnp.dot(
            gx_ref[start : start + rows, :],
            half_ref[slot, low : low + width, :],
            preferred_element_type=jnp.float32,
        )
        finish(start, rows, acc)


def fill_moments(src_ref, count, mu_ref, inv_ref, gx_ref, gy_ref, half_ref, blocks, width, begin=0):
    def step(r, _):
        x = src_ref[r]
        half_ref[0] = jnp.dot(x, gy_ref[...], preferred_element_type=jnp.float32).astype(
            jnp.bfloat16
        )
        half_ref[1] = jnp.dot(x * x, gy_ref[...], preferred_element_type=jnp.float32).astype(
            jnp.bfloat16
        )
        for start, rows, low in blocks:
            gx = gx_ref[start : start + rows, :]
            mu = jnp.dot(
                gx, half_ref[0, low : low + width, :], preferred_element_type=jnp.float32
            )
            sq = jnp.dot(
                gx, half_ref[1, low : low + width, :], preferred_element_type=jnp.float32
            )
            mu_ref[r, start : start + rows, :] = mu
            inv_ref[r, start : start + rows, :] = lax.rsqrt(jnp.abs(sq - mu * mu + 0.1))
        return 0

    lax.fori_loop(begin, count, step, 0)


def fill_pairs(
    runs, src_ref, far_ref, mu_a, inv_a, mu_b, inv_b, gx_ref, gy_ref,
    half_ref, stage, sems, sums_ref, ncc_ref, blocks, width, count, early=None, base=0,
):
    total = runs[-1][0] + runs[-1][4]
    steps = total // BATCH
    assert steps * BATCH == total and steps >= 2

    def decode(q):
        slot, place, s = jnp.int32(0), jnp.int32(0), jnp.int32(0)
        for first, run_slot, run_place, low, _ in runs:
            here = q >= first
            slot = jnp.where(here, run_slot, slot)
            place = jnp.where(here, run_place, place)
            s = jnp.where(here, low + q - first, s)
        return slot, s, place - s

    def copy(bank, b, s, d):
        return pltpu.make_async_copy(
            stage.at[bank * BATCH + b], ncc_ref.at[s, d - 1], sems.at[bank * BATCH + b]
        )

    def step(t, _):
        bank = lax.rem(t, 2)
        which = [decode(t * BATCH + b) for b in range(BATCH)]

        if early is None:

            @pl.when(t >= 2)
            def _():
                for b in range(BATCH):
                    copy(bank, b, 0, 1).wait()

        for b, (slot, s, d) in enumerate(which):
            half_ref[b] = jnp.dot(
                src_ref[s] * far_ref[slot], gy_ref[...], preferred_element_type=jnp.float32
            ).astype(jnp.bfloat16)
        for b, (slot, s, d) in enumerate(which):
            parts = []

            def finish(start, rows, acc):
                at = slice(start, start + rows)
                ncc = (acc - mu_a[s, at, :] * mu_b[slot, at, :]) * (
                    inv_a[s, at, :] * inv_b[slot, at, :]
                )
                if early is None:
                    stage[bank * BATCH + b, at, :] = ncc.astype(jnp.bfloat16)
                else:
                    early[base + t * BATCH + b, at, :] = ncc.astype(jnp.bfloat16)
                    parts.append(jnp.sum(ncc.reshape(rows // 8, 8, ncc.shape[1]), axis=0))

            blur_to(half_ref, gx_ref, blocks, width, b, finish)
            if early is None:
                copy(bank, b, s, d).start()
            else:
                sums_ref[jnp.where(d == 1, s, count)] = functools.reduce(jnp.add, parts)
        return 0

    lax.fori_loop(0, steps, step, 0)
    if early is not None:
        return
    for bank in range(2):
        for b in range(BATCH):
            copy(bank, b, 0, 1).wait()


def first_kernel(
    blocks, width, groups, count, devices, pixels,
    radius_ref, src_ref,
    early_ref, far_ref, mu_ref, inv_ref, gx_ref, gy_ref, out_ref,
    mu_far, inv_far, half_ref, sums_ref, mine, slots,
    halo_send, halo_recv, send_sems, recv_sems,
):
    me = lax.axis_index("gz")
    mesh_id = pl.DeviceIdType.MESH
    barrier = pltpu.get_barrier_semaphore()
    peers = [lax.rem(me + k, devices) for k in range(1, devices)]
    for peer in peers:
        pl.semaphore_signal(barrier, inc=1, device_id={"gz": peer}, device_id_type=mesh_id)
    for start, rows, low in blocks:
        gx_ref[start : start + rows, :] = table(radius_ref[0], (rows, width), start, low, 1)
    gy_ref[...] = table(radius_ref[1], gy_ref.shape, 0, 0, 0)
    half = count // 2
    fill_moments(src_ref, half, mu_ref, inv_ref, gx_ref, gy_ref, half_ref, blocks, width)
    pl.semaphore_wait(barrier, devices - 1)
    halo = [
        pltpu.make_async_remote_copy(
            src_ref=src_ref.at[j],
            dst_ref=far_ref.at[j],
            send_sem=halo_send.at[j],
            recv_sem=halo_recv.at[j],
            device_id={"gz": lax.rem(me + devices - 1, devices)},
            device_id_type=mesh_id,
        )
        for j in range(REACH)
    ]

    @pl.when(me > 0)
    def _():
        for copy in halo:
            copy.start()

    def arrive(a, b):
        @pl.when(me < devices - 1)
        def _():
            for j in range(a, b):
                halo[j].wait_recv()

        @pl.when(me == devices - 1)
        def _():
            for j in range(a, b):
                far_ref[j] = jnp.zeros(far_ref.shape[1:], far_ref.dtype)

    fill_moments(src_ref, count, mu_ref, inv_ref, gx_ref, gy_ref, half_ref, blocks, width, half)
    base, copies, running = 0, [], None
    for a, b, runs in groups:
        if b == 0:
            source, mu_b, inv_b = src_ref, mu_ref, inv_ref
        else:
            arrive(a, b)
            source, mu_b, inv_b = far_ref.at[pl.ds(a, b - a)], mu_far, inv_far
            fill_moments(
                source, b - a, mu_far, inv_far, gx_ref, gy_ref, half_ref, blocks, width
            )
        fill_pairs(
            runs, src_ref, source, mu_ref, inv_ref, mu_b, inv_b, gx_ref, gy_ref,
            half_ref, None, None, sums_ref, None, blocks, width, count, early_ref, base,
        )
        base += runs[-1][0] + runs[-1][4]
        if b == 1:
            sums = jnp.sum(jnp.sum(sums_ref[:count], axis=1), axis=1, keepdims=True)
            row = lax.broadcasted_iota(jnp.int32, (count, LANES), 0)
            lane = lax.broadcasted_iota(jnp.int32, (count, LANES), 1)
            spacing = 1.25 - jnp.broadcast_to(sums, (count, LANES)) / pixels
            mine[...] = jnp.broadcast_to(jnp.sum(spacing, axis=0, keepdims=True), mine.shape)
            running = jnp.sum(jnp.where(row <= lane, spacing, 0.0), axis=0, keepdims=True)
            for k, peer in enumerate(peers, 1):
                copy = pltpu.make_async_remote_copy(
                    src_ref=mine,
                    dst_ref=slots.at[k],
                    send_sem=send_sems.at[k],
                    recv_sem=recv_sems.at[k],
                    device_id={"gz": peer},
                    device_id_type=mesh_id,
                )
                copy.start()
                copies.append(copy)
    arrive(groups[-1][1], REACH)

    @pl.when(me > 0)
    def _():
        for copy in halo:
            copy.wait_send()

    for copy in copies:
        copy.wait()
    for k in range(1, devices):
        running = running + jnp.where(k <= me, slots[k, :1, :], 0.0)
    out_ref[...] = running * 0.015625


def last_kernel(
    blocks, width, groups, runs, begin, count,
    src_ref, far_ref, mu_ref, inv_ref, gx_ref, gy_ref, early_ref,
    ncc_ref,
    mu_far, inv_far, half_ref, stage, sems, early_sems,
):
    copies = []
    for _, _, done in groups:
        for _, _, place, low, number in done:
            for s in range(low, low + number):
                q = len(copies)
                copy = pltpu.make_async_copy(
                    early_ref.at[q], ncc_ref.at[s, place - s - 1], early_sems.at[q]
                )
                copy.start()
                copies.append(copy)
    source = far_ref.at[pl.ds(begin, REACH - begin)]
    fill_moments(
        source, REACH - begin, mu_far, inv_far, gx_ref, gy_ref, half_ref, blocks, width
    )
    fill_pairs(
        runs, src_ref, source, mu_ref, inv_ref, mu_far, inv_far, gx_ref, gy_ref,
        half_ref, stage, sems, None, ncc_ref, blocks, width, count,
    )
    for copy in copies:
        copy.wait()


def make_runs(places, count):
    out = []
    first = 0
    for slot, place in places:
        low, high = max(0, place - REACH), min(place, count)
        if high > low:
            out.append((first, slot, place, low, high - low))
            first += high - low
    return out


def per_device(sections, radius):
    count, tx, ty = sections.shape
    width, blocks = windows(tx)
    axis = lax.axis_size("gz")
    vmem = pl.BlockSpec(memory_space=pltpu.VMEM)
    smem = pl.BlockSpec(memory_space=pltpu.SMEM)
    hbm = pl.BlockSpec(memory_space=pl.ANY)
    shape = jax.ShapeDtypeStruct
    map_type = shape((count, tx, ty), jnp.float32)
    groups = [(0, 0, make_runs([(p, p) for p in range(count)], count))]
    for a, b in ((0, 1), (1, LATE)):
        groups.append((a, b, make_runs([(j - a, count + j) for j in range(a, b)], count)))
    late = make_runs([(j - LATE, count + j) for j in range(LATE, REACH)], count)
    pairs = sum(runs[-1][0] + runs[-1][4] for _, _, runs in groups)
    dma = pltpu.SemaphoreType.DMA
    early, far, mu, inv, gx, gy, positions = pl.pallas_call(
        functools.partial(first_kernel, blocks, width, groups, count, axis, tx * ty),
        out_shape=(
            shape((pairs, tx, ty), jnp.bfloat16),
            shape((REACH, tx, ty), jnp.bfloat16),
            map_type, map_type,
            shape((tx, width), jnp.bfloat16), shape((ty, ty), jnp.bfloat16),
            shape((1, LANES), jnp.float32),
        ),
        in_specs=[smem, vmem],
        out_specs=[vmem] * 7,
        scratch_shapes=[pltpu.VMEM((LATE - 1, tx, ty), jnp.float32)] * 2
        + [
            pltpu.VMEM((2, tx, ty), jnp.bfloat16),
            pltpu.VMEM((count + 1, 8, ty), jnp.float32),
            pltpu.VMEM((8, LANES), jnp.float32),
            pltpu.VMEM((axis, 8, LANES), jnp.float32),
            dma((REACH,)), dma((REACH,)), dma((axis,)), dma((axis,)),
        ],
        compiler_params=pltpu.CompilerParams(
            collective_id=0, has_side_effects=True, vmem_limit_bytes=FIRST_LIMIT
        ),
        name="first_pairs",
    )(radius, sections)
    ncc = pl.pallas_call(
        functools.partial(last_kernel, blocks, width, groups, late, LATE, count),
        out_shape=shape((count, REACH, tx, ty), jnp.bfloat16),
        in_specs=[vmem] * 6 + [hbm],
        out_specs=hbm,
        scratch_shapes=[pltpu.VMEM((REACH - LATE, tx, ty), jnp.float32)] * 2
        + [
            pltpu.VMEM((2, tx, ty), jnp.bfloat16),
            pltpu.VMEM((2 * BATCH, tx, ty), jnp.bfloat16),
            dma((2 * BATCH,)), dma((pairs,)),
        ],
        compiler_params=pltpu.CompilerParams(vmem_limit_bytes=LAST_LIMIT),
        name="last_pairs",
    )(sections, far, mu, inv, gx, gy, early)
    return (ncc, positions[0, :count])


def solution(mesh):
    in_specs = (P(("grp", "gz"), None, None), P())
    out_specs = (P(("grp", "gz"), None, None, None), P(("grp", "gz")))
    return jax.shard_map(
        per_device, mesh=mesh, in_specs=in_specs, out_specs=out_specs, check_vma=False
    )
```
